32 devices in a mesh: groups: 1, mp: 4 (over x, core), dp: 8 (over z, y).
Axes of the slice: x: 2, y: 2, z: 4, core: 2. Of those that a mesh axis runs over, the one named last changes fastest.
Arguments:
- stream: bfloat16 [1024, 4608], P(('groups', 'mp'), 'dp'), may hold values from -12 to 12
- active_lists: int32 [8, 8], P(('groups', 'mp')), may hold values from -1 to 63, as said below
- enc_weight: bfloat16 [4608, 8192], P('dp', 'mp'), may hold values from -0.09375 to 0.09375
- enc_bias: float32 [8192], P('mp'), may hold values from -3 to 3
- dec_weight: bfloat16 [8192, 4608], P('mp', 'dp'), may hold values from -0.25 to 0.25
- dec_bias: float32 [4608], P('dp'), may hold values from -3 to 3
Outputs:
- grad_enc: bfloat16 [4608, 8192], P(('groups', 'dp'), 'mp')
- grad_enc_bias: float32 [8192], P(('groups', 'mp'))
- grad_dec: bfloat16 [8192, 4608], P(('groups', 'mp'), 'dp')
- errors: bfloat16 [1024, 4608], P(('groups', 'mp'), 'dp')
The draws below stay inside these ranges and needn't reach their ends.
Inputs may be any that keep to these rules, and one draw needn't show every extreme that they name: `active_lists`: each row names distinct latent blocks; -1 marks an unused entry. Over the rows of one index of mp, at most 8 entries name blocks of one model shard (blocks k * 16 to (k + 1) * 16 - 1), and in every draw some model shard is named exactly 8 times by the rows of every index of mp.
All inputs are finite; a program needn't handle non-finite values.
Results may differ from the reference program's by a relative error of at most 0.0131.
Values may be sent and summed in bfloat16 or wider, within the bound.
A program may use at most 128 MiB of HBM per device.

```python
import jax
import jax.numpy as jnp
from jax import lax

D = 4608
BLK = 128
TB = 128
LIST = 8
LBLK_DEV = 16
TOK_DEV = 256
TOKENS = 1024
LATENTS = 8192
CAP = 8
N_MP = 4


def draw_stream(key, part):
    key = jax.random.fold_in(key, 7)
    key_main, key_rows = jax.random.split(key, 2)
    ramp_scale = jnp.sqrt(1.0 + 2.0 * jnp.arange(TOKENS, dtype=jnp.float32) / TOKENS)[:, None]
    base_draw = jax.random.normal(key_main, (TOKENS, D), jnp.float32)
    row_scale = jnp.exp(jax.random.uniform(key_rows, (TOKENS, 1), jnp.float32, -0.35, 0.35))
    values_drawn = base_draw * ramp_scale * row_scale
    return jnp.clip(values_drawn, -12.0, 12.0).astype(jnp.bfloat16)


def draw_active_lists(key, part):
    key = jax.random.fold_in(key, 11)
    home_blocks = TOK_DEV // TB
    home_slots = LIST * home_blocks
    hot_shard = jax.random.randint(jax.random.fold_in(key, 1), (), 0, N_MP)

    def one_home(home_key):
        key_pick, key_order, key_base, key_drop = jax.random.split(home_key, 4)
        others = jnp.arange((N_MP - 1) * CAP) // CAP
        others = others + (others >= hot_shard).astype(jnp.int32)
        picked = others[jax.random.permutation(key_pick, (N_MP - 1) * CAP)][:home_slots - CAP]
        owners = jnp.concatenate([jnp.full((CAP,), hot_shard, jnp.int32), picked.astype(jnp.int32)])
        owners = owners[jax.random.permutation(key_order, home_slots)].reshape(home_blocks, LIST)
        base_draw = jax.random.randint(key_base, (home_blocks, 1), 0, LBLK_DEV)
        local_id = (base_draw + jnp.arange(LIST)[None, :]) % LBLK_DEV
        block_ids = owners * LBLK_DEV + local_id
        dropped = (jax.random.randint(key_drop, (home_blocks, LIST), 0, 4) == 0) & (owners != hot_shard)
        return jnp.where(dropped, -1, block_ids)
    homes = jax.vmap(one_home)(jax.random.split(jax.random.fold_in(key, 2), N_MP))
    return homes.reshape(home_blocks * N_MP, LIST).astype(jnp.int32)


def level_of(rng, dims, pieces, least, high):
    def one(dim, parts):
        steps = jax.random.uniform(jax.random.fold_in(jax.random.fold_in(rng, 6), dim), (parts,), jnp.float32, least / len(pieces), high / len(pieces))
        return jnp.repeat(jnp.exp(steps), dims[dim] // parts).reshape((-1,) + (1,) * (len(dims) - dim - 1))

    level = one(*pieces[0])
    for cut in pieces[1:]:
        level = level * one(*cut)
    return level


def noise(own_key, extent, scale, most, shards=(), held_as=jnp.bfloat16):
    drawn = jax.random.normal(own_key, extent, jnp.float32) * scale
    if len(shards) > 0:
        drawn = level_of(own_key, extent, shards, -0.22, 0.18) * drawn
    return jnp.clip(drawn, min=-most, max=most).astype(held_as)


def setup_inputs(seed: int = 0, part: int = 0) -> dict:
    arg_keys = jax.random.split(jax.random.key(seed), 7)
    part_splits = jax.random.split(jax.random.fold_in(arg_keys[6], part), 7)
    return {
        "stream": draw_stream(jax.random.fold_in(jax.random.fold_in(arg_keys[6], part), 71), part),
        "active_lists": draw_active_lists(jax.random.fold_in(jax.random.fold_in(arg_keys[6], part), 71), part),
        "enc_weight": noise(arg_keys[2], (D, LATENTS), D ** -0.5, 0.09375, ((0, 8), (1, 4))),
        "enc_bias": noise(arg_keys[3], (LATENTS,), 0.5, 3.0, ((0, 4),), jnp.float32),
        "dec_weight": noise(arg_keys[4], (LATENTS, D), (4 * BLK) ** -0.5, 0.25, ((0, 4), (1, 8))),
        "dec_bias": noise(arg_keys[5], (D,), 0.5, 3.0, ((0, 8),), jnp.float32),
    }


def reference(stream, active_lists, enc_weight, enc_bias, dec_weight, dec_bias):
    block_total = LATENTS // BLK
    token_blocks = TOKENS // TB
    highest = lax.Precision.HIGHEST
    stream_blocks = stream.reshape(token_blocks, TB, D)
    enc_blocks = enc_weight.reshape(D, block_total, BLK)
    dec_blocks = dec_weight.reshape(block_total, BLK, D)
    bias_blocks = enc_bias.reshape(block_total, BLK)

    def step(carry, inputs):
        acc_enc, acc_dec, acc_bias = carry
        token_rows, list_row = inputs
        is_live = list_row >= 0
        block_id = jnp.where(is_live, list_row, 0).astype(jnp.int32)
        rows_wide = token_rows.astype(jnp.float32)
        enc_sel = jnp.take(enc_blocks, block_id, axis=1).astype(jnp.float32)
        dec_sel = jnp.take(dec_blocks, block_id, axis=0).astype(jnp.float32)
        bias_sel = jnp.take(bias_blocks, block_id, axis=0)
        pre = jnp.einsum('td,dsb->stb', rows_wide, enc_sel, precision=highest) + bias_sel[:, None, :]
        keep = is_live[:, None, None] & (pre > 0)
        latents = jnp.where(keep, pre, 0.0).astype(jnp.bfloat16)
        latents_wide = latents.astype(jnp.float32)
        dec_part = jnp.einsum('stb,sbd->std', latents_wide, dec_sel, precision=highest).astype(jnp.bfloat16)
        recon = jnp.sum(dec_part.astype(jnp.float32), axis=0) + dec_bias[None, :]
        errors = (recon - rows_wide).astype(jnp.bfloat16)
        errors_wide = errors.astype(jnp.float32)
        code_grad = jnp.einsum('td,sbd->stb', errors_wide, dec_sel, precision=highest)
        pre_grad = jnp.where(latents > 0, code_grad / TB, 0.0).astype(jnp.bfloat16)
        pre_grad_wide = pre_grad.astype(jnp.float32)
        add_dec = jnp.einsum('stb,td->sbd', latents_wide, errors_wide, precision=highest)
        add_enc = jnp.einsum('td,stb->sdb', rows_wide, pre_grad_wide, precision=highest)
        add_bias = jnp.sum(pre_grad_wide, axis=1)
        acc_enc = acc_enc.at[block_id].add(add_enc)
        acc_dec = acc_dec.at[block_id].add(add_dec)
        acc_bias = acc_bias.at[block_id].add(add_bias)
        return (acc_enc, acc_dec, acc_bias), errors

    start_state = (jnp.zeros((block_total, D, BLK), jnp.float32),
                   jnp.zeros((block_total, BLK, D), jnp.float32),
                   jnp.zeros((block_total, BLK), jnp.float32))
    (acc_enc, acc_dec, acc_bias), all_errors = lax.scan(step, start_state, (stream_blocks, active_lists))
    grad_enc = jnp.transpose(acc_enc, (1, 0, 2)).reshape(D, LATENTS).astype(jnp.bfloat16)
    grad_dec = (acc_dec / TB).reshape(LATENTS, D).astype(jnp.bfloat16)
    return grad_enc, acc_bias.reshape(LATENTS), grad_dec, all_errors.reshape(TOKENS, D)
```

```python
import functools

import jax
import jax.numpy as jnp
from jax import lax
from jax.experimental import pallas as pl
from jax.experimental.pallas import tpu as pltpu
from jax.sharding import PartitionSpec as P

BLK = 128
TB = 128
LIST = 8
LBLK_DEV = 16
F32 = jnp.float32
BF16 = jnp.bfloat16
VMEM_BYTES = 48 * 1024 * 1024


class Axis:
    def __init__(self, name, size):
        self.name = name
        self.fars = size // 2
        self.me = lax.axis_index(name)
        self.far = self.me // 2
        self.near = self.me % 2

    def later(self, step):
        return lax.rem(self.far + step, self.fars)

    def index(self, far, near):
        return 2 * far + near

    def sibling(self):
        return self.index(self.far, 1 - self.near)

    def push(self, src, dst, send, recv, target):
        return pltpu.make_async_remote_copy(
            src_ref=src,
            dst_ref=dst,
            send_sem=send,
            recv_sem=recv,
            device_id={self.name: target},
            device_id_type=pl.DeviceIdType.MESH,
        )

    def greet(self, barrier):
        pl.semaphore_signal(
            barrier, inc=1, device_id={self.name: self.sibling()}, device_id_type=pl.DeviceIdType.MESH
        )
        for step in range(1, self.fars):
            pl.semaphore_signal(
                barrier,
                inc=1,
                device_id={self.name: self.index(self.later(step), self.near)},
                device_id_type=pl.DeviceIdType.MESH,
            )
        return self.fars


def gather_start(ax, buf, rows, sems):
    far_send, far_recv, near_send, near_recv = sems
    mine = buf.at[pl.ds(ax.me * rows, rows)]
    copies = []
    for step in range(1, ax.fars):
        peer = ax.later(step)
        copies.append(
            ax.push(mine, mine, far_send.at[peer], far_recv.at[ax.far], ax.index(peer, ax.near))
        )
    copies.append(ax.push(mine, mine, near_send.at[ax.far], near_recv.at[ax.far], ax.sibling()))
    for copy in copies:
        copy.start()
    return copies


def gather_finish(ax, buf, rows, sems, copies):
    far_send, far_recv, near_send, near_recv = sems
    for step in range(1, ax.fars):
        peer = ax.later(ax.fars - step)
        landed = buf.at[pl.ds(ax.index(peer, ax.near) * rows, rows)]
        ax.push(
            landed, landed, far_send.at[peer], far_recv.at[peer], ax.index(peer, ax.near)
        ).wait_recv()
        copy = ax.push(landed, landed, near_send.at[peer], near_recv.at[peer], ax.sibling())
        copy.start()
        copies.append(copy)
    for step in range(ax.fars):
        peer = ax.later(ax.fars - step)
        landed = buf.at[pl.ds(ax.index(peer, 1 - ax.near) * rows, rows)]
        ax.push(
            landed, landed, near_send.at[peer], near_recv.at[peer], ax.sibling()
        ).wait_recv()
    for copy in copies:
        copy.wait_send()


def scatter_sum(ax, produce, away, own, near_in, pair, far_in, sems):
    far_send, far_recv, near_send, near_recv = sems
    copies = []
    for step in range(1, ax.fars + 1):
        peer = ax.later(step)
        produce(ax.index(peer, 1 - ax.near), away, peer)
        copy = ax.push(
            away.at[peer], near_in.at[peer], near_send.at[peer], near_recv.at[peer], ax.sibling()
        )
        copy.start()
        copies.append(copy)
    for step in range(1, ax.fars + 1):
        produce(ax.index(ax.later(step), ax.near), own, ax.later(step))

    def wait_near(peer):
        ax.push(
            near_in.at[peer], near_in.at[peer], near_send.at[peer], near_recv.at[peer], ax.sibling()
        ).wait_recv()

    for step in range(1, ax.fars):
        peer = ax.later(step)
        wait_near(peer)
        pair[peer] = (own[peer] + near_in[peer].astype(F32)).astype(pair.dtype)
        copy = ax.push(
            pair.at[peer],
            far_in.at[ax.far],
            far_send.at[peer],
            far_recv.at[ax.far],
            ax.index(peer, ax.near),
        )
        copy.start()
        copies.append(copy)
    wait_near(ax.far)
    total = own[ax.far] + near_in[ax.far].astype(F32)
    for step in range(1, ax.fars):
        peer = ax.later(ax.fars - step)
        ax.push(
            far_in.at[peer],
            far_in.at[peer],
            far_send.at[peer],
            far_recv.at[peer],
            ax.index(peer, ax.near),
        ).wait_recv()
        total = total + far_in[peer].astype(F32)
    for copy in copies:
        copy.wait_send()
    return total


def gather_kernel(
    n_mp, rows, stream_ref, list_ref, enc_ref, stream_out, list_out, enc_out, buf, lists, *sems
):
    ax = Axis("mp", n_mp)
    barrier = pltpu.get_barrier_semaphore()
    pl.semaphore_wait(barrier, ax.greet(barrier))
    buf[pl.ds(ax.me * rows, rows)] = stream_ref[...]
    lists[pl.ds(ax.me, 1)] = list_ref[...]
    list_copies = gather_start(ax, lists, 1, sems[4:8])
    copies = gather_start(ax, buf, rows, sems[0:4])
    for k in range(LBLK_DEV):
        enc_out[k] = enc_ref[:, k * BLK:(k + 1) * BLK]
    gather_finish(ax, lists, 1, sems[4:8], list_copies)
    gather_finish(ax, buf, rows, sems[0:4], copies)
    stream_out[...] = buf[...]
    list_out[...] = lists[...]


def main_kernel(
    n_mp, n_dp, rows, cap,
    table, hits, stream, enc, dec, enc_bias, dec_bias,
    lat_out, pg_out, err_all_out, err_out,
    lat, pg, err, picked, picked_dec,
    pre_away, pre_own, pre_near, pre_pair, pre_far,
    dec_away, dec_own, dec_near, dec_pair, dec_far,
    code_away, code_own, code_near, code_pair, code_far,
    *sems,
):
    mp = Axis("mp", n_mp)
    dp = Axis("dp", n_dp)
    per = n_mp * cap // n_dp
    barrier = pltpu.get_barrier_semaphore()
    count = mp.greet(barrier) + dp.greet(barrier)
    pl.semaphore_wait(barrier, count)

    def group(i):
        return sems[4 * i:4 * i + 4]

    def produce_pre(chunk, dest, place):
        def one(i, _):
            slot = chunk * per + i
            dest[place, i] = jnp.dot(
                stream[table[0, slot]], enc[table[1, slot]], preferred_element_type=F32
            )
            return 0

        lax.fori_loop(0, per, one, 0)

    pre_sum = scatter_sum(
        dp, produce_pre, pre_away, pre_own, pre_near, pre_pair, pre_far, group(0)
    )
    for i in range(per):
        slot = dp.me * per + i
        shifted = pre_sum[i] + enc_bias[table[1, slot]]
        live = jnp.sum(hits[slot], axis=0, keepdims=True)
        lat[slot] = (jnp.maximum(shifted, 0.0) * live).astype(BF16)
    gather_finish(dp, lat, per, group(1), gather_start(dp, lat, per, group(1)))

    def produce_dec(home, dest, place):
        for c in range(cap):
            slot = home * cap + c
            picked_dec[c * BLK:(c + 1) * BLK, :] = dec[table[1, slot]]
            block = lat[slot]
            for j in range(rows):
                hit = jnp.broadcast_to(hits[slot, j:j + 1], (TB, BLK)).astype(BF16)
                picked[j * TB:(j + 1) * TB, c * BLK:(c + 1) * BLK] = block * hit
        out = jnp.dot(picked[...], picked_dec[...], preferred_element_type=F32)
        dest[place] = out.reshape(dest.shape[1:]).astype(dest.dtype)

    recon = scatter_sum(
        mp, produce_dec, dec_away, dec_own, dec_near, dec_pair, dec_far, group(2)
    )
    recon = recon + dec_bias[...][None]
    mine = (recon - stream[pl.ds(mp.me * rows, rows)].astype(F32)).astype(BF16)
    err[pl.ds(mp.me * rows, rows)] = mine
    copies = gather_start(mp, err, rows, group(3))
    err_out[...] = mine
    lat_out[...] = lat[...]
    gather_finish(mp, err, rows, group(3), copies)

    def produce_code(chunk, dest, place):
        def one(i, _):
            slot = chunk * per + i
            dest[place, i] = lax.dot_general(
                err[table[0, slot]],
                dec[table[1, slot]],
                (((1,), (1,)), ((), ())),
                preferred_element_type=F32,
            ).astype(dest.dtype)
            return 0

        lax.fori_loop(0, per, one, 0)

    code = scatter_sum(
        dp, produce_code, code_away, code_own, code_near, code_pair, code_far, group(4)
    )
    for i in range(per):
        slot = dp.me * per + i
        on = lat[slot].astype(F32) > 0
        pg[slot] = jnp.where(on, code[i] * (1.0 / TB), 0.0).astype(BF16)
    copies = gather_start(dp, pg, per, group(5))
    err_all_out[...] = err[...]
    gather_finish(dp, pg, per, group(5), copies)
    pg_out[...] = pg[...]


def grad_kernel(
    slots, table, stream, err, lat, pg, genc, gbias, gdec, acc_enc, acc_dec
):
    acc_enc[...] = jnp.zeros_like(acc_enc)
    acc_dec[...] = jnp.zeros_like(acc_dec)
    gbias[...] = jnp.zeros_like(gbias)
    contract = (((0,), (0,)), ((), ()))

    def one(slot, _):
        block, where = table[0, slot], table[1, slot]
        pg_block = pg[slot]
        acc_dec[where] += lax.dot_general(
            lat[slot], err[block], contract, preferred_element_type=F32
        )
        acc_enc[where] += lax.dot_general(
            stream[block], pg_block, contract, preferred_element_type=F32
        )
        gbias[pl.ds(where, 1), :] += jnp.sum(pg_block.astype(F32), axis=0, keepdims=True)
        return 0

    lax.fori_loop(0, slots, one, 0)
    for k in range(LBLK_DEV):
        genc[:, k * BLK:(k + 1) * BLK] = acc_enc[k].astype(BF16)
        gdec[k] = (acc_dec[k] * (1.0 / TB)).astype(BF16)


def local(n_mp, n_dp, stream, active_lists, enc_weight, enc_bias, dec_weight, dec_bias):
    tok_count, feat = stream.shape
    rows = tok_count // TB
    cap = max(2, 16 * rows // n_mp)
    slots = n_mp * cap
    per = slots // n_dp
    blocks = n_mp * rows
    mps, dps = n_mp // 2, n_dp // 2
    vmem = pl.BlockSpec(memory_space=pltpu.VMEM)
    smem = pl.BlockSpec(memory_space=pltpu.SMEM)
    dma = pltpu.SemaphoreType.DMA
    shape = jax.ShapeDtypeStruct

    lists = jnp.full((1, 8, 128), -1, jnp.int32).at[0, :rows, :LIST].set(active_lists)
    stream_all, lists_all, enc_blocks = pl.pallas_call(
        functools.partial(gather_kernel, n_mp, rows),
        out_shape=(
            shape((blocks, TB, feat), BF16),
            shape((n_mp, 8, 128), jnp.int32),
            shape((LBLK_DEV, feat, BLK), BF16),
        ),
        in_specs=[vmem] * 3,
        out_specs=(vmem,) * 3,
        scratch_shapes=[
            pltpu.VMEM((blocks, TB, feat), BF16),
            pltpu.VMEM((n_mp, 8, 128), jnp.int32),
        ] + [dma((mps,))] * 8,
        compiler_params=pltpu.CompilerParams(
            collective_id=0, has_side_effects=True, vmem_limit_bytes=VMEM_BYTES
        ),
    )(stream.reshape(rows, TB, feat), lists, enc_weight)

    ids = lists_all[:, :rows, :LIST].reshape(n_mp, rows * LIST)
    entry = jnp.arange(rows * LIST)
    mine = (ids >= 0) & (ids // LBLK_DEV == lax.axis_index("mp"))
    before = jnp.sum(mine[:, None, :] & (entry[None, :] < entry[:, None])[None], axis=2)
    placed = mine[:, None, :] & (before[:, None, :] == jnp.arange(cap)[None, :, None])
    home = jnp.arange(n_mp)[:, None, None] * rows
    table = jnp.stack([
        jnp.sum(jnp.where(placed, entry // LIST, 0), axis=2) + home[:, :, 0],
        jnp.sum(jnp.where(placed, (ids % LBLK_DEV)[:, None, :], 0), axis=2),
    ]).reshape(2, slots).astype(jnp.int32)
    in_row = (entry // LIST)[None, :] == jnp.arange(rows)[:, None]
    hits = jnp.sum((placed[:, :, None, :] & in_row).astype(F32), axis=3)
    hits = jnp.broadcast_to(hits.reshape(slots, rows, 1), (slots, rows, BLK))

    small = (TB, BLK)
    wide = (rows, TB, feat)
    lat, pg, err_all, errors = pl.pallas_call(
        functools.partial(main_kernel, n_mp, n_dp, rows, cap),
        out_shape=(
            shape((slots,) + small, BF16),
            shape((slots,) + small, BF16),
            shape((blocks, TB, feat), BF16),
            shape(wide, BF16),
        ),
        in_specs=[smem] + [vmem] * 6,
        out_specs=(vmem,) * 4,
        scratch_shapes=[
            pltpu.VMEM((slots,) + small, BF16),
            pltpu.VMEM((slots,) + small, BF16),
            pltpu.VMEM((blocks, TB, feat), BF16),
            pltpu.VMEM((tok_count, cap * BLK), BF16),
            pltpu.VMEM((cap * BLK, feat), BF16),
        ]
        + [pltpu.VMEM((dps, per) + small, F32)] * 5
        + [pltpu.VMEM((mps,) + wide, t) for t in (BF16, F32, BF16, BF16, BF16)]
        + [pltpu.VMEM((dps, per) + small, t) for t in (BF16, F32, BF16, BF16, BF16)]
        + [dma((dps,))] * 8 + [dma((mps,))] * 8 + [dma((dps,))] * 8,
        compiler_params=pltpu.CompilerParams(
            collective_id=1, has_side_effects=True, vmem_limit_bytes=VMEM_BYTES
        ),
    )(
        table,
        hits,
        stream_all,
        enc_blocks,
        dec_weight.reshape(LBLK_DEV, BLK, feat),
        enc_bias.reshape(LBLK_DEV, 1, BLK),
        dec_bias.reshape(1, feat),
    )

    grad_enc, grad_bias, grad_dec = pl.pallas_call(
        functools.partial(grad_kernel, slots),
        out_shape=(
            shape((feat, LBLK_DEV * BLK), BF16),
            shape((LBLK_DEV, BLK), F32),
            shape((LBLK_DEV, BLK, feat), BF16),
        ),
        in_specs=[smem] + [vmem] * 4,
        out_specs=(vmem,) * 3,
        scratch_shapes=[
            pltpu.VMEM((LBLK_DEV, feat, BLK), F32),
            pltpu.VMEM((LBLK_DEV, BLK, feat), F32),
        ],
        compiler_params=pltpu.CompilerParams(vmem_limit_bytes=VMEM_BYTES),
    )(table, stream_all, err_all, lat, pg)
    return (
        grad_enc,
        grad_bias.reshape(LBLK_DEV * BLK),
        grad_dec.reshape(LBLK_DEV * BLK, feat),
        errors.reshape(tok_count, feat),
    )


def solution(mesh):
    return jax.shard_map(
        functools.partial(local, mesh.shape["mp"], mesh.shape["dp"]),
        mesh=mesh,
        in_specs=(
            P(("groups", "mp"), "dp"),
            P(("groups", "mp"), None),
            P("dp", "mp"),
            P("mp"),
            P("mp", "dp"),
            P("dp"),
        ),
        out_specs=(
            P(("groups", "dp"), "mp"),
            P(("groups", "mp")),
            P(("groups", "mp"), "dp"),
            P(("groups", "mp"), "dp"),
        ),
        check_vma=False,
    )
```

```python
import functools

import jax
import jax.numpy as jnp
from jax import lax
from jax.experimental import pallas as pl
from jax.experimental.pallas import tpu as pltpu
from jax.sharding import PartitionSpec as P

BLK = 128
TB = 128
LIST = 8
LBLK_DEV = 16
F32 = jnp.float32
BF16 = jnp.bfloat16
VMEM_BYTES = 48 * 1024 * 1024


class Axis:
    def __init__(self, name, size):
        self.name = name
        self.fars = size // 2
        self.me = lax.axis_index(name)
        self.far = self.me // 2
        self.near = self.me % 2

    def later(self, step):
        return lax.rem(self.far + step, self.fars)

    def index(self, far, near):
        return 2 * far + near

    def sibling(self):
        return self.index(self.far, 1 - self.near)

    def push(self, src, dst, send, recv, target):
        return pltpu.make_async_remote_copy(
            src_ref=src,
            dst_ref=dst,
            send_sem=send,
            recv_sem=recv,
            device_id={self.name: target},
            device_id_type=pl.DeviceIdType.MESH,
        )

    def greet(self, barrier):
        pl.semaphore_signal(
            barrier, inc=1, device_id={self.name: self.sibling()}, device_id_type=pl.DeviceIdType.MESH
        )
        for step in range(1, self.fars):
            pl.semaphore_signal(
                barrier,
                inc=1,
                device_id={self.name: self.index(self.later(step), self.near)},
                device_id_type=pl.DeviceIdType.MESH,
            )
        return self.fars


def gather_start(ax, buf, rows, sems):
    far_send, far_recv, near_send, near_recv = sems
    mine = buf.at[pl.ds(ax.me * rows, rows)]
    copies = []
    for step in range(1, ax.fars):
        peer = ax.later(step)
        copies.append(
            ax.push(mine, mine, far_send.at[peer], far_recv.at[ax.far], ax.index(peer, ax.near))
        )
    copies.append(ax.push(mine, mine, near_send.at[ax.far], near_recv.at[ax.far], ax.sibling()))
    for copy in copies:
        copy.start()
    return copies


def gather_finish(ax, buf, rows, sems, copies, work=lambda step: None):
    far_send, far_recv, near_send, near_recv = sems
    work(0)
    for step in range(1, ax.fars):
        peer = ax.later(ax.fars - step)
        landed = buf.at[pl.ds(ax.index(peer, ax.near) * rows, rows)]
        ax.push(
            landed, landed, far_send.at[peer], far_recv.at[peer], ax.index(peer, ax.near)
        ).wait_recv()
        copy = ax.push(landed, landed, near_send.at[peer], near_recv.at[peer], ax.sibling())
        copy.start()
        copies.append(copy)
        work(step)
    for step in range(ax.fars):
        peer = ax.later(ax.fars - step)
        landed = buf.at[pl.ds(ax.index(peer, 1 - ax.near) * rows, rows)]
        ax.push(
            landed, landed, near_send.at[peer], near_recv.at[peer], ax.sibling()
        ).wait_recv()
    for copy in copies:
        copy.wait_send()


def scatter_sum(ax, produce, away, own, near_in, pair, far_in, sems):
    far_send, far_recv, near_send, near_recv = sems
    copies = []
    for step in range(1, ax.fars + 1):
        peer = ax.later(step)
        produce(ax.index(peer, 1 - ax.near), away, peer)
        copy = ax.push(
            away.at[peer], near_in.at[peer], near_send.at[peer], near_recv.at[peer], ax.sibling()
        )
        copy.start()
        copies.append(copy)
    for step in range(1, ax.fars + 1):
        produce(ax.index(ax.later(step), ax.near), own, ax.later(step))

    def wait_near(peer):
        ax.push(
            near_in.at[peer], near_in.at[peer], near_send.at[peer], near_recv.at[peer], ax.sibling()
        ).wait_recv()

    for step in range(1, ax.fars):
        peer = ax.later(step)
        wait_near(peer)
        pair[peer] = (own[peer] + near_in[peer].astype(F32)).astype(pair.dtype)
        copy = ax.push(
            pair.at[peer],
            far_in.at[ax.far],
            far_send.at[peer],
            far_recv.at[ax.far],
            ax.index(peer, ax.near),
        )
        copy.start()
        copies.append(copy)
    wait_near(ax.far)
    total = own[ax.far] + near_in[ax.far].astype(F32)
    for step in range(1, ax.fars):
        peer = ax.later(ax.fars - step)
        ax.push(
            far_in.at[peer],
            far_in.at[peer],
            far_send.at[peer],
            far_recv.at[peer],
            ax.index(peer, ax.near),
        ).wait_recv()
        total = total + far_in[peer].astype(F32)
    for copy in copies:
        copy.wait_send()
    return total


def gather_kernel(
    n_mp, rows, stream_ref, list_ref, enc_ref, dec_ref,
    stream_out, list_out, enc_out, dec_out, buf, lists, *sems
):
    ax = Axis("mp", n_mp)
    barrier = pltpu.get_barrier_semaphore()
    greeted = ax.greet(barrier)
    for j in range(rows):
        buf[ax.me * rows + j] = stream_ref[:, j * TB:(j + 1) * TB].T
    pl.semaphore_wait(barrier, greeted)
    lists[pl.ds(ax.me, 1)] = list_ref[...]
    list_copies = gather_start(ax, lists, 1, sems[4:8])
    copies = gather_start(ax, buf, rows, sems[0:4])
    for k in range(LBLK_DEV):
        enc_out[k] = enc_ref[:, k * BLK:(k + 1) * BLK]
        dec_out[k] = dec_ref[:, k * BLK:(k + 1) * BLK].T
    gather_finish(ax, lists, 1, sems[4:8], list_copies)
    gather_finish(ax, buf, rows, sems[0:4], copies)
    stream_out[...] = buf[...]
    list_out[...] = lists[...]


def spread_pair(blocks, pair, where, held, spread):
    for b in range(blocks):
        for i in range(2):
            spread[b * TB:(b + 1) * TB, i * BLK:(i + 1) * BLK] = held[where[b, 2 * pair + i]]


def main_kernel(
    n_mp, n_dp, rows, cap,
    table, where, hits, stream, enc, dec, enc_bias, dec_bias,
    pg_out, stream_out, gdec_out, err_out,
    lat, pg, err, picked, picked_dec, err_wide, spread,
    pre_away, pre_own, pre_near, pre_pair, pre_far,
    dec_away, dec_own, dec_near, dec_pair, dec_far,
    code_away, code_own, code_near, code_pair, code_far,
    *sems,
):
    mp = Axis("mp", n_mp)
    dp = Axis("dp", n_dp)
    per = n_mp * cap // n_dp
    barrier = pltpu.get_barrier_semaphore()
    count = mp.greet(barrier) + dp.greet(barrier)
    empty = jnp.zeros((TB, BLK), BF16)
    lat[n_mp * cap] = empty
    pg[n_mp * cap] = empty
    pl.semaphore_wait(barrier, count)

    def group(i):
        return sems[4 * i:4 * i + 4]

    def produce_pre(chunk, dest, place):
        def one(i, _):
            slot = chunk * per + i
            dest[place, i] = jnp.dot(
                stream[table[0, slot]], enc[table[1, slot]], preferred_element_type=F32
            )
            return 0

        lax.fori_loop(0, per, one, 0)

    pre_sum = scatter_sum(
        dp, produce_pre, pre_away, pre_own, pre_near, pre_pair, pre_far, group(0)
    )
    for i in range(per):
        slot = dp.me * per + i
        shifted = pre_sum[i] + enc_bias[table[1, slot]]
        live = jnp.sum(hits[slot], axis=0, keepdims=True)
        lat[slot] = (jnp.maximum(shifted, 0.0) * live).astype(BF16)
    gather_finish(dp, lat, per, group(1), gather_start(dp, lat, per, group(1)))

    def produce_dec(home, dest, place):
        for c in range(cap):
            slot = home * cap + c
            picked_dec[c * BLK:(c + 1) * BLK, :] = dec[table[1, slot]]
            block = lat[slot]
            for j in range(rows):
                hit = jnp.broadcast_to(hits[slot, j:j + 1], (TB, BLK)).astype(BF16)
                picked[j * TB:(j + 1) * TB, c * BLK:(c + 1) * BLK] = block * hit
        out = jnp.dot(picked[...], picked_dec[...], preferred_element_type=F32)
        dest[place] = out.reshape(dest.shape[1:]).astype(dest.dtype)

    recon = scatter_sum(
        mp, produce_dec, dec_away, dec_own, dec_near, dec_pair, dec_far, group(2)
    )
    recon = recon + dec_bias[...][None]
    mine = (recon - stream[pl.ds(mp.me * rows, rows)].astype(F32)).astype(BF16)
    err[pl.ds(mp.me * rows, rows)] = mine
    copies = gather_start(mp, err, rows, group(3))
    for j in range(rows):
        err_out[:, j * TB:(j + 1) * TB] = mine[j].T
    for b in range(n_mp * rows):
        stream_out[:, b * TB:(b + 1) * TB] = stream[b].T
    gather_finish(mp, err, rows, group(3), copies)

    def produce_code(chunk, dest, place):
        def one(i, _):
            slot = chunk * per + i
            dest[place, i] = lax.dot_general(
                err[table[0, slot]],
                dec[table[1, slot]],
                (((1,), (1,)), ((), ())),
                preferred_element_type=F32,
            ).astype(dest.dtype)
            return 0

        lax.fori_loop(0, per, one, 0)

    code = scatter_sum(
        dp, produce_code, code_away, code_own, code_near, code_pair, code_far, group(4)
    )
    for i in range(per):
        slot = dp.me * per + i
        on = lat[slot].astype(F32) > 0
        pg[slot] = jnp.where(on, code[i] * (1.0 / TB), 0.0).astype(BF16)
    copies = gather_start(dp, pg, per, group(5))
    blocks = n_mp * rows
    for b in range(blocks):
        err_wide[:, b * TB:(b + 1) * TB] = err[b].T
    share = LBLK_DEV // 2 // dp.fars

    def grad_dec(step):
        def one(pair, _):
            spread_pair(blocks, pair, where, lat, spread)
            total = jnp.dot(err_wide[...], spread[...], preferred_element_type=F32)
            lane = pl.multiple_of(pair * 2 * BLK, 2 * BLK)
            gdec_out[:, pl.ds(lane, 2 * BLK)] = (total * (1.0 / TB)).astype(BF16)
            return 0

        lax.fori_loop(step * share, (step + 1) * share, one, 0)

    gather_finish(dp, pg, per, group(5), copies, grad_dec)
    pg_out[...] = pg[...]


def grad_kernel(blocks, where, stream, pg, genc, gbias, spread):
    spread_pair(blocks, pl.program_id(0), where, pg, spread)
    genc[...] = jnp.dot(stream[...], spread[...], preferred_element_type=F32).astype(BF16)
    gbias[...] = jnp.sum(spread[...].astype(F32), axis=0, keepdims=True)


def local(n_mp, n_dp, stream, active_lists, enc_weight, enc_bias, dec_weight, dec_bias):
    tok_count, feat = stream.shape
    rows = tok_count // TB
    cap = max(2, 16 * rows // n_mp)
    slots = n_mp * cap
    per = slots // n_dp
    blocks = n_mp * rows
    mps, dps = n_mp // 2, n_dp // 2
    vmem = pl.BlockSpec(memory_space=pltpu.VMEM)
    smem = pl.BlockSpec(memory_space=pltpu.SMEM)
    dma = pltpu.SemaphoreType.DMA
    shape = jax.ShapeDtypeStruct

    lists = jnp.full((1, 8, 128), -1, jnp.int32).at[0, :rows, :LIST].set(active_lists)
    stream_all, lists_all, enc_blocks, dec_blocks = pl.pallas_call(
        functools.partial(gather_kernel, n_mp, rows),
        out_shape=(
            shape((blocks, TB, feat), BF16),
            shape((n_mp, 8, 128), jnp.int32),
            shape((LBLK_DEV, feat, BLK), BF16),
            shape((LBLK_DEV, BLK, feat), BF16),
        ),
        in_specs=[vmem] * 4,
        out_specs=(vmem,) * 4,
        scratch_shapes=[
            pltpu.VMEM((blocks, TB, feat), BF16),
            pltpu.VMEM((n_mp, 8, 128), jnp.int32),
        ] + [dma((mps,))] * 8,
        compiler_params=pltpu.CompilerParams(
            collective_id=0, has_side_effects=True, vmem_limit_bytes=VMEM_BYTES
        ),
    )(stream.T, lists, enc_weight, dec_weight.T)

    ids = lists_all[:, :rows, :LIST].reshape(n_mp, rows * LIST)
    entry = jnp.arange(rows * LIST)
    mine = (ids >= 0) & (ids // LBLK_DEV == lax.axis_index("mp"))
    before = jnp.sum(mine[:, None, :] & (entry[None, :] < entry[:, None])[None], axis=2)
    placed = mine[:, None, :] & (before[:, None, :] == jnp.arange(cap)[None, :, None])
    home = jnp.arange(n_mp)[:, None, None] * rows
    table = jnp.stack([
        jnp.sum(jnp.where(placed, entry // LIST, 0), axis=2) + home[:, :, 0],
        jnp.sum(jnp.where(placed, (ids % LBLK_DEV)[:, None, :], 0), axis=2),
    ]).reshape(2, slots).astype(jnp.int32)
    in_row = (entry // LIST)[None, :] == jnp.arange(rows)[:, None]
    hits = jnp.sum((placed[:, :, None, :] & in_row).astype(F32), axis=3)
    hits = jnp.broadcast_to(hits.reshape(slots, rows, 1), (slots, rows, BLK))

    held = placed[:, :, None, :] & in_row
    held = held[..., None] & (ids % LBLK_DEV == jnp.arange(LBLK_DEV)[:, None, None]).transpose(1, 2, 0)[
        :, None, None
    ]
    number = jnp.arange(slots).reshape(n_mp, cap, 1, 1, 1)
    where = slots - jnp.sum(jnp.where(held, slots - number, 0), axis=(1, 3))
    where = where.reshape(blocks, LBLK_DEV).astype(jnp.int32)

    small = (TB, BLK)
    wide = (rows, TB, feat)
    pg, stream_wide, grad_dec, errors = pl.pallas_call(
        functools.partial(main_kernel, n_mp, n_dp, rows, cap),
        out_shape=(
            shape((slots + 1,) + small, BF16),
            shape((feat, blocks * TB), BF16),
            shape((feat, LBLK_DEV * BLK), BF16),
            shape((feat, tok_count), BF16),
        ),
        in_specs=[smem] * 2 + [vmem] * 6,
        out_specs=(vmem,) * 4,
        scratch_shapes=[
            pltpu.VMEM((slots + 1,) + small, BF16),
            pltpu.VMEM((slots + 1,) + small, BF16),
            pltpu.VMEM((blocks, TB, feat), BF16),
            pltpu.VMEM((tok_count, cap * BLK), BF16),
            pltpu.VMEM((cap * BLK, feat), BF16),
            pltpu.VMEM((feat, blocks * TB), BF16),
            pltpu.VMEM((blocks * TB, 2 * BLK), BF16),
        ]
        + [pltpu.VMEM((dps, per) + small, F32)] * 5
        + [pltpu.VMEM((mps,) + wide, t) for t in (BF16, F32, BF16, BF16, BF16)]
        + [pltpu.VMEM((dps, per) + small, t) for t in (BF16, F32, BF16, BF16, BF16)]
        + [dma((dps,))] * 8 + [dma((mps,))] * 8 + [dma((dps,))] * 8,
        compiler_params=pltpu.CompilerParams(
            collective_id=1, has_side_effects=True, vmem_limit_bytes=VMEM_BYTES
        ),
    )(
        table,
        where,
        hits,
        stream_all,
        enc_blocks,
        dec_blocks,
        enc_bias.reshape(LBLK_DEV, 1, BLK),
        dec_bias.reshape(1, feat),
    )

    grad_enc, grad_bias = pl.pallas_call(
        functools.partial(grad_kernel, blocks),
        grid=(LBLK_DEV // 2,),
        out_shape=(
            shape((feat, LBLK_DEV * BLK), BF16),
            shape((1, LBLK_DEV * BLK), F32),
        ),
        in_specs=[smem] + [vmem] * 2,
        out_specs=(
            pl.BlockSpec((feat, 2 * BLK), lambda i: (0, i)),
            pl.BlockSpec((1, 2 * BLK), lambda i: (0, i)),
        ),
        scratch_shapes=[pltpu.VMEM((blocks * TB, 2 * BLK), BF16)],
        compiler_params=pltpu.CompilerParams(vmem_limit_bytes=VMEM_BYTES),
    )(where, stream_wide, pg)
    return (grad_enc, grad_bias.reshape(LBLK_DEV * BLK), grad_dec.T, errors.T)


def solution(mesh):
    return jax.shard_map(
        functools.partial(local, mesh.shape["mp"], mesh.shape["dp"]),
        mesh=mesh,
        in_specs=(
            P(("groups", "mp"), "dp"),
            P(("groups", "mp"), None),
            P("dp", "mp"),
            P("mp"),
            P("mp", "dp"),
            P("dp"),
        ),
        out_specs=(
            P(("groups", "dp"), "mp"),
            P(("groups", "mp")),
            P(("groups", "mp"), "dp"),
            P(("groups", "mp"), "dp"),
        ),
        check_vma=False,
    )
```

```python
import functools

import jax
import jax.numpy as jnp
from jax import lax
from jax.experimental import pallas as pl
from jax.experimental.pallas import tpu as pltpu
from jax.sharding import PartitionSpec as P

BLK = 128
TB = 128
LIST = 8
LBLK_DEV = 16
F32 = jnp.float32
BF16 = jnp.bfloat16
VMEM_BYTES = 48 * 1024 * 1024


class Axis:
    def __init__(self, name, size):
        self.name = name
        self.fars = size // 2
        self.me = lax.axis_index(name)
        self.far = self.me // 2
        self.near = self.me % 2

    def later(self, step):
        return lax.rem(self.far + step, self.fars)

    def index(self, far, near):
        return 2 * far + near

    def sibling(self):
        return self.index(self.far, 1 - self.near)

    def push(self, src, dst, send, recv, target):
        return pltpu.make_async_remote_copy(
            src_ref=src,
            dst_ref=dst,
            send_sem=send,
            recv_sem=recv,
            device_id={self.name: target},
            device_id_type=pl.DeviceIdType.MESH,
        )

    def greet(self, barrier):
        pl.semaphore_signal(
            barrier, inc=1, device_id={self.name: self.sibling()}, device_id_type=pl.DeviceIdType.MESH
        )
        for step in range(1, self.fars):
            pl.semaphore_signal(
                barrier,
                inc=1,
                device_id={self.name: self.index(self.later(step), self.near)},
                device_id_type=pl.DeviceIdType.MESH,
            )
        return self.fars


def gather_start(ax, buf, region, sems, pending):
    far_send, far_recv, near_send, near_recv = sems
    mine = buf.at[region(ax.me)]
    copies = []
    for step in range(1, ax.fars):
        peer = ax.later(step)
        copies.append(
            ax.push(mine, mine, far_send.at[peer], far_recv.at[ax.far], ax.index(peer, ax.near))
        )
    copies.append(ax.push(mine, mine, near_send.at[ax.far], near_recv.at[ax.far], ax.sibling()))
    for copy in copies:
        copy.start()
    pending.extend(copies)


def gather_finish(ax, buf, region, sems, pending, work=lambda step: None):
    far_send, far_recv, near_send, near_recv = sems
    work(0)
    for step in range(1, ax.fars):
        peer = ax.later(ax.fars - step)
        landed = buf.at[region(ax.index(peer, ax.near))]
        ax.push(
            landed, landed, far_send.at[peer], far_recv.at[peer], ax.index(peer, ax.near)
        ).wait_recv()
        copy = ax.push(landed, landed, near_send.at[peer], near_recv.at[peer], ax.sibling())
        copy.start()
        pending.append(copy)
        work(step)
    for step in range(ax.fars):
        peer = ax.later(ax.fars - step)
        landed = buf.at[region(ax.index(peer, 1 - ax.near))]
        ax.push(
            landed, landed, near_send.at[peer], near_recv.at[peer], ax.sibling()
        ).wait_recv()


def scatter_sum(ax, produce, bufs, sems, pending):
    away, own, near_in, pair, far_in = bufs
    far_send, far_recv, near_send, near_recv = sems
    for step in range(1, ax.fars + 1):
        peer = ax.later(step)
        produce(ax.index(peer, 1 - ax.near), away, peer)
        copy = ax.push(
            away.at[peer], near_in.at[peer], near_send.at[peer], near_recv.at[peer], ax.sibling()
        )
        copy.start()
        pending.append(copy)
    yield

    def wait_near(peer):
        ax.push(
            near_in.at[peer], near_in.at[peer], near_send.at[peer], near_recv.at[peer], ax.sibling()
        ).wait_recv()

    for step in range(1, ax.fars):
        peer = ax.later(step)
        produce(ax.index(peer, ax.near), own, peer)
        wait_near(peer)
        pair[peer] = (own[peer] + near_in[peer].astype(F32)).astype(pair.dtype)
        copy = ax.push(
            pair.at[peer],
            far_in.at[ax.far],
            far_send.at[peer],
            far_recv.at[ax.far],
            ax.index(peer, ax.near),
        )
        copy.start()
        pending.append(copy)
    produce(ax.me, own, ax.far)
    yield
    wait_near(ax.far)
    total = own[ax.far] + near_in[ax.far].astype(F32)
    for step in range(1, ax.fars):
        peer = ax.later(ax.fars - step)
        ax.push(
            far_in.at[peer],
            far_in.at[peer],
            far_send.at[peer],
            far_recv.at[peer],
            ax.index(peer, ax.near),
        ).wait_recv()
        total = total + far_in[peer].astype(F32)
    yield total


def gather_kernel(
    n_mp, rows, stream_ref, list_ref, enc_ref,
    stream_out, list_out, enc_out, buf, lists, *sems
):
    ax = Axis("mp", n_mp)
    barrier = pltpu.get_barrier_semaphore()
    greeted = ax.greet(barrier)
    for j in range(rows):
        buf[ax.me * rows + j] = stream_ref[:, j * TB:(j + 1) * TB].T
    pl.semaphore_wait(barrier, greeted)
    lists[pl.ds(ax.me, 1)] = list_ref[...]
    pending = []

    def one_list(m):
        return pl.ds(m, 1)

    def home(m):
        return pl.ds(m * rows, rows)

    gather_start(ax, lists, one_list, sems[4:8], pending)
    gather_start(ax, buf, home, sems[0:4], pending)
    for k in range(LBLK_DEV):
        enc_out[k] = enc_ref[:, k * BLK:(k + 1) * BLK]
    gather_finish(ax, lists, one_list, sems[4:8], pending)
    gather_finish(ax, buf, home, sems[0:4], pending)
    for copy in pending:
        copy.wait_send()
    stream_out[...] = buf[...]
    list_out[...] = lists[...]


def spread_pair(blocks, pair, where, held, spread):
    for b in range(blocks):
        for i in range(2):
            spread[b * TB:(b + 1) * TB, i * BLK:(i + 1) * BLK] = held[where[b, 2 * pair + i]]


def main_kernel(
    n_mp, n_dp, rows, cap, parts,
    table, where, hits, stream, enc, dec_in, enc_bias, dec_bias,
    pg_out, stream_out, gdec_out, err_out,
    lat, pg, err, dec, dec_wide, picked, picked_dec, err_wide, spread, *rest,
):
    mp = Axis("mp", n_mp)
    dp = Axis("dp", n_dp)
    per = n_mp * cap // n_dp
    part = per // parts
    blocks = n_mp * rows
    pre_bufs, dec_bufs, code_bufs, sems = rest[0:5], rest[5:10], rest[10:15], rest[15:]
    barrier = pltpu.get_barrier_semaphore()
    count = mp.greet(barrier) + dp.greet(barrier)
    empty = jnp.zeros((TB, BLK), BF16)
    lat[n_mp * cap] = empty
    pg[n_mp * cap] = empty
    pl.semaphore_wait(barrier, count)
    pending = []

    def group(i):
        return sems[4 * i:4 * i + 4]

    def home_rows(m):
        return pl.ds(m * rows, rows)

    def region(p):
        return lambda m: pl.ds(m * per + p * part, part)

    def producer(p, left, right):
        def produce(chunk, dest, place):
            def one(i, _):
                slot = chunk * per + p * part + i
                dest[place, i] = jnp.dot(
                    left[table[0, slot]], right[table[1, slot]], preferred_element_type=F32
                ).astype(dest.dtype)
                return 0

            lax.fori_loop(0, part, one, 0, unroll=True)

        return produce

    def reduce_and_gather(left, right, bufs, first, held, finish, aside, work):
        sums = [
            scatter_sum(
                dp,
                producer(p, left, right),
                [b.at[p] for b in bufs],
                group(first + p),
                pending,
            )
            for p in range(parts)
        ]
        for p in range(parts):
            next(sums[p])
        for p in range(parts):
            next(sums[p])
            aside(p)
        for p in range(parts):
            total = next(sums[p])
            for i in range(part):
                slot = dp.me * per + p * part + i
                held[slot] = finish(slot, total[i])
            gather_start(dp, held, region(p), group(first + parts + p), pending)
        for p in range(parts):
            gather_finish(
                dp, held, region(p), group(first + parts + p), pending, functools.partial(work, p)
            )

    def activate(slot, pre_sum):
        shifted = pre_sum + enc_bias[table[1, slot]]
        live = jnp.sum(hits[slot], axis=0, keepdims=True)
        return (jnp.maximum(shifted, 0.0) * live).astype(BF16)

    def turn_dec(p):
        for k in range(p * LBLK_DEV // parts, (p + 1) * LBLK_DEV // parts):
            dec[k] = dec_in[:, k * BLK:(k + 1) * BLK].T

    def split_dec(p, step):
        calls = parts * dp.fars
        at = p * dp.fars + step
        for k in range(at * LBLK_DEV // calls, (at + 1) * LBLK_DEV // calls):
            dec_wide[k] = dec_in[:, k * BLK:(k + 1) * BLK]

    reduce_and_gather(stream, enc, pre_bufs, 0, lat, activate, turn_dec, split_dec)

    def produce_dec(home, dest, place):
        for c in range(cap):
            slot = home * cap + c
            picked_dec[c * BLK:(c + 1) * BLK, :] = dec[table[1, slot]]
            block = lat[slot]
            for j in range(rows):
                hit = jnp.broadcast_to(hits[slot, j:j + 1], (TB, BLK)).astype(BF16)
                picked[j * TB:(j + 1) * TB, c * BLK:(c + 1) * BLK] = block * hit
        out = jnp.dot(picked[...], picked_dec[...], preferred_element_type=F32)
        dest[place] = out.reshape(dest.shape[1:]).astype(dest.dtype)

    sums = scatter_sum(mp, produce_dec, dec_bufs, group(4 * parts), pending)
    next(sums)
    next(sums)
    recon = next(sums) + dec_bias[...][None]
    mine = (recon - stream[home_rows(mp.me)].astype(F32)).astype(BF16)
    err[home_rows(mp.me)] = mine
    gather_start(mp, err, home_rows, group(4 * parts + 1), pending)
    for j in range(rows):
        err_out[:, j * TB:(j + 1) * TB] = mine[j].T
    for b in range(blocks):
        stream_out[:, b * TB:(b + 1) * TB] = stream[b].T
    gather_finish(mp, err, home_rows, group(4 * parts + 1), pending)

    def to_pre_grad(slot, code):
        on = lat[slot].astype(F32) > 0
        return jnp.where(on, code * (1.0 / TB), 0.0).astype(BF16)

    def turn_err(p):
        for b in range(p * blocks // parts, (p + 1) * blocks // parts):
            err_wide[:, b * TB:(b + 1) * TB] = err[b].T

    def grad_dec(p, step):
        calls = parts * dp.fars
        at = p * dp.fars + step
        pairs = LBLK_DEV // 2

        def one(pair, _):
            spread_pair(blocks, pair, where, lat, spread)
            total = jnp.dot(err_wide[...], spread[...], preferred_element_type=F32)
            lane = pl.multiple_of(pair * 2 * BLK, 2 * BLK)
            gdec_out[:, pl.ds(lane, 2 * BLK)] = (total * (1.0 / TB)).astype(BF16)
            return 0

        if at * pairs // calls < (at + 1) * pairs // calls:
            lax.fori_loop(at * pairs // calls, (at + 1) * pairs // calls, one, 0)

    reduce_and_gather(err, dec_wide, code_bufs, 2 * parts, pg, to_pre_grad, turn_err, grad_dec)
    pg_out[...] = pg[...]
    for copy in pending:
        copy.wait_send()


def grad_kernel(blocks, where, stream, pg, gdec_in, err_in, genc, gbias, gdec, err, spread):
    gdec[...] = gdec_in[...]

    @pl.when(pl.program_id(0) == 0)
    def _():
        err[...] = err_in[...]

    spread_pair(blocks, pl.program_id(0), where, pg, spread)
    genc[...] = jnp.dot(stream[...], spread[...], preferred_element_type=F32).astype(BF16)
    gbias[...] = jnp.sum(spread[...].astype(F32), axis=0, keepdims=True)


def local(n_mp, n_dp, stream, active_lists, enc_weight, enc_bias, dec_weight, dec_bias):
    tok_count, feat = stream.shape
    rows = tok_count // TB
    cap = max(2, 16 * rows // n_mp)
    slots = n_mp * cap
    per = slots // n_dp
    parts = 2 if per % 2 == 0 else 1
    chunk = (parts, n_dp // 2, per // parts, TB, BLK)
    blocks = n_mp * rows
    mps, dps = n_mp // 2, n_dp // 2
    vmem = pl.BlockSpec(memory_space=pltpu.VMEM)
    smem = pl.BlockSpec(memory_space=pltpu.SMEM)
    dma = pltpu.SemaphoreType.DMA
    shape = jax.ShapeDtypeStruct

    lists = jnp.full((1, 8, 128), -1, jnp.int32).at[0, :rows, :LIST].set(active_lists)
    stream_all, lists_all, enc_blocks = pl.pallas_call(
        functools.partial(gather_kernel, n_mp, rows),
        out_shape=(
            shape((blocks, TB, feat), BF16),
            shape((n_mp, 8, 128), jnp.int32),
            shape((LBLK_DEV, feat, BLK), BF16),
        ),
        in_specs=[vmem] * 3,
        out_specs=(vmem,) * 3,
        scratch_shapes=[
            pltpu.VMEM((blocks, TB, feat), BF16),
            pltpu.VMEM((n_mp, 8, 128), jnp.int32),
        ] + [dma((mps,))] * 8,
        compiler_params=pltpu.CompilerParams(
            collective_id=0, has_side_effects=True, vmem_limit_bytes=VMEM_BYTES
        ),
    )(stream.T, lists, enc_weight)

    ids = lists_all[:, :rows, :LIST].reshape(n_mp, rows * LIST)
    entry = jnp.arange(rows * LIST)
    mine = (ids >= 0) & (ids // LBLK_DEV == lax.axis_index("mp"))
    before = jnp.sum(mine[:, None, :] & (entry[None, :] < entry[:, None])[None], axis=2)
    placed = mine[:, None, :] & (before[:, None, :] == jnp.arange(cap)[None, :, None])
    home = jnp.arange(n_mp)[:, None, None] * rows
    table = jnp.stack([
        jnp.sum(jnp.where(placed, entry // LIST, 0), axis=2) + home[:, :, 0],
        jnp.sum(jnp.where(placed, (ids % LBLK_DEV)[:, None, :], 0), axis=2),
    ]).reshape(2, slots).astype(jnp.int32)
    in_row = (entry // LIST)[None, :] == jnp.arange(rows)[:, None]
    hits = jnp.sum((placed[:, :, None, :] & in_row).astype(F32), axis=3)
    hits = jnp.broadcast_to(hits.reshape(slots, rows, 1), (slots, rows, BLK))

    held = placed[:, :, None, :] & in_row
    held = held[..., None] & (ids % LBLK_DEV == jnp.arange(LBLK_DEV)[:, None, None]).transpose(1, 2, 0)[
        :, None, None
    ]
    number = jnp.arange(slots).reshape(n_mp, cap, 1, 1, 1)
    where = slots - jnp.sum(jnp.where(held, slots - number, 0), axis=(1, 3))
    where = where.reshape(blocks, LBLK_DEV).astype(jnp.int32)

    small = (TB, BLK)
    wide = (rows, TB, feat)
    pg, stream_wide, grad_dec, errors = pl.pallas_call(
        functools.partial(main_kernel, n_mp, n_dp, rows, cap, parts),
        out_shape=(
            shape((slots + 1,) + small, BF16),
            shape((feat, blocks * TB), BF16),
            shape((feat, LBLK_DEV * BLK), BF16),
            shape((feat, tok_count), BF16),
        ),
        in_specs=[smem] * 2 + [vmem] * 6,
        out_specs=(vmem,) * 4,
        scratch_shapes=[
            pltpu.VMEM((slots + 1,) + small, BF16),
            pltpu.VMEM((slots + 1,) + small, BF16),
            pltpu.VMEM((blocks, TB, feat), BF16),
            pltpu.VMEM((LBLK_DEV, BLK, feat), BF16),
            pltpu.VMEM((LBLK_DEV, feat, BLK), BF16),
            pltpu.VMEM((tok_count, cap * BLK), BF16),
            pltpu.VMEM((cap * BLK, feat), BF16),
            pltpu.VMEM((feat, blocks * TB), BF16),
            pltpu.VMEM((blocks * TB, 2 * BLK), BF16),
        ]
        + [pltpu.VMEM(chunk, F32)] * 5
        + [pltpu.VMEM((mps,) + wide, t) for t in (BF16, F32, BF16, BF16, BF16)]
        + [pltpu.VMEM(chunk, t) for t in (BF16, F32, BF16, BF16, BF16)]
        + [dma((dps,))] * (16 * parts) + [dma((mps,))] * 8,
        compiler_params=pltpu.CompilerParams(
            collective_id=1, has_side_effects=True, vmem_limit_bytes=VMEM_BYTES
        ),
    )(
        table,
        where,
        hits,
        stream_all,
        enc_blocks,
        dec_weight.T,
        enc_bias.reshape(LBLK_DEV, 1, BLK),
        dec_bias.reshape(1, feat),
    )

    pair = pl.BlockSpec((feat, 2 * BLK), lambda i: (0, i))
    whole = pl.BlockSpec((feat, tok_count), lambda i: (0, 0))
    grad_enc, grad_bias, grad_dec, errors = pl.pallas_call(
        functools.partial(grad_kernel, blocks),
        grid=(LBLK_DEV // 2,),
        out_shape=(
            shape((feat, LBLK_DEV * BLK), BF16),
            shape((1, LBLK_DEV * BLK), F32),
            shape((feat, LBLK_DEV * BLK), BF16),
            shape((feat, tok_count), BF16),
        ),
        in_specs=[smem] + [vmem] * 2 + [pair, whole],
        out_specs=(pair, pl.BlockSpec((1, 2 * BLK), lambda i: (0, i)), pair, whole),
        scratch_shapes=[pltpu.VMEM((blocks * TB, 2 * BLK), BF16)],
        compiler_params=pltpu.CompilerParams(vmem_limit_bytes=VMEM_BYTES),
    )(where, stream_wide, pg, grad_dec, errors)
    return (grad_enc, grad_bias.reshape(LBLK_DEV * BLK), grad_dec.T, errors.T)


def solution(mesh):
    return jax.shard_map(
        functools.partial(local, mesh.shape["mp"], mesh.shape["dp"]),
        mesh=mesh,
        in_specs=(
            P(("groups", "mp"), "dp"),
            P(("groups", "mp"), None),
            P("dp", "mp"),
            P("mp"),
            P("mp", "dp"),
            P("dp"),
        ),
        out_specs=(
            P(("groups", "dp"), "mp"),
            P(("groups", "mp")),
            P(("groups", "mp"), "dp"),
            P(("groups", "mp"), "dp"),
        ),
        check_vma=False,
    )
```

```python
import functools

import jax
import jax.numpy as jnp
from jax import lax
from jax.experimental import pallas as pl
from jax.experimental.pallas import tpu as pltpu
from jax.sharding import PartitionSpec as P

BLK = 128
TB = 128
LIST = 8
LBLK_DEV = 16
F32 = jnp.float32
BF16 = jnp.bfloat16
VMEM_BYTES = 48 * 1024 * 1024


class Axis:
    def __init__(self, name, size):
        self.name = name
        self.fars = size // 2
        self.me = lax.axis_index(name)
        self.far = self.me // 2
        self.near = self.me % 2

    def later(self, step):
        return lax.rem(self.far + step, self.fars)

    def index(self, far, near):
        return 2 * far + near

    def sibling(self):
        return self.index(self.far, 1 - self.near)

    def push(self, src, dst, send, recv, target):
        return pltpu.make_async_remote_copy(
            src_ref=src,
            dst_ref=dst,
            send_sem=send,
            recv_sem=recv,
            device_id={self.name: target},
            device_id_type=pl.DeviceIdType.MESH,
        )

    def greet(self, barrier):
        pl.semaphore_signal(
            barrier, inc=1, device_id={self.name: self.sibling()}, device_id_type=pl.DeviceIdType.MESH
        )
        for step in range(1, self.fars):
            pl.semaphore_signal(
                barrier,
                inc=1,
                device_id={self.name: self.index(self.later(step), self.near)},
                device_id_type=pl.DeviceIdType.MESH,
            )
        return self.fars


def gather_start(ax, buf, region, sems, pending):
    far_send, far_recv, near_send, near_recv = sems
    mine = buf.at[region(ax.me)]
    copies = []
    for step in range(1, ax.fars):
        peer = ax.later(step)
        copies.append(
            ax.push(mine, mine, far_send.at[peer], far_recv.at[ax.far], ax.index(peer, ax.near))
        )
    copies.append(ax.push(mine, mine, near_send.at[ax.far], near_recv.at[ax.far], ax.sibling()))
    for copy in copies:
        copy.start()
    pending.extend(copies)


def gather_forward(ax, buf, region, sems, pending, work=lambda step: None):
    far_send, far_recv, near_send, near_recv = sems
    work(0)
    for step in range(1, ax.fars):
        peer = ax.later(ax.fars - step)
        landed = buf.at[region(ax.index(peer, ax.near))]
        ax.push(
            landed, landed, far_send.at[peer], far_recv.at[peer], ax.index(peer, ax.near)
        ).wait_recv()
        copy = ax.push(landed, landed, near_send.at[peer], near_recv.at[peer], ax.sibling())
        copy.start()
        pending.append(copy)
        work(step)


def gather_finish(ax, buf, region, sems):
    far_send, far_recv, near_send, near_recv = sems
    for step in range(ax.fars):
        peer = ax.later(ax.fars - step)
        landed = buf.at[region(ax.index(peer, 1 - ax.near))]
        ax.push(
            landed, landed, near_send.at[peer], near_recv.at[peer], ax.sibling()
        ).wait_recv()


def scatter_sum(ax, produce, bufs, sems, pending):
    away, own, near_in, pair, far_in = bufs
    far_send, far_recv, near_send, near_recv = sems
    for step in range(1, ax.fars + 1):
        peer = ax.later(step)
        produce(ax.index(peer, 1 - ax.near), away, peer)
        copy = ax.push(
            away.at[peer], near_in.at[peer], near_send.at[peer], near_recv.at[peer], ax.sibling()
        )
        copy.start()
        pending.append(copy)
        yield

    def wait_near(peer):
        ax.push(
            near_in.at[peer], near_in.at[peer], near_send.at[peer], near_recv.at[peer], ax.sibling()
        ).wait_recv()

    for step in range(1, ax.fars):
        peer = ax.later(step)
        produce(ax.index(peer, ax.near), own, peer)
        wait_near(peer)
        pair[peer] = (own[peer] + near_in[peer].astype(F32)).astype(pair.dtype)
        copy = ax.push(
            pair.at[peer],
            far_in.at[ax.far],
            far_send.at[peer],
            far_recv.at[ax.far],
            ax.index(peer, ax.near),
        )
        copy.start()
        pending.append(copy)
        yield
    produce(ax.me, own, ax.far)
    yield
    wait_near(ax.far)
    total = own[ax.far] + near_in[ax.far].astype(F32)
    for step in range(1, ax.fars):
        peer = ax.later(ax.fars - step)
        ax.push(
            far_in.at[peer],
            far_in.at[peer],
            far_send.at[peer],
            far_recv.at[peer],
            ax.index(peer, ax.near),
        ).wait_recv()
        total = total + far_in[peer].astype(F32)
    yield total


def gather_kernel(
    n_mp, rows, stream_ref, list_ref, enc_ref,
    stream_out, list_out, enc_out, buf, lists, *sems
):
    ax = Axis("mp", n_mp)
    barrier = pltpu.get_barrier_semaphore()
    greeted = ax.greet(barrier)
    for j in range(rows):
        buf[ax.me * rows + j] = stream_ref[:, j * TB:(j + 1) * TB].T
    pl.semaphore_wait(barrier, greeted)
    lists[pl.ds(ax.me, 1)] = list_ref[...]
    pending = []

    def one_list(m):
        return pl.ds(m, 1)

    def home(m):
        return pl.ds(m * rows, rows)

    gather_start(ax, lists, one_list, sems[4:8], pending)
    gather_start(ax, buf, home, sems[0:4], pending)
    for k in range(LBLK_DEV):
        enc_out[k] = enc_ref[:, k * BLK:(k + 1) * BLK]
    gather_forward(ax, lists, one_list, sems[4:8], pending)
    gather_forward(ax, buf, home, sems[0:4], pending)
    gather_finish(ax, lists, one_list, sems[4:8])
    gather_finish(ax, buf, home, sems[0:4])
    for copy in pending:
        copy.wait_send()
    stream_out[...] = buf[...]
    list_out[...] = lists[...]


def spread_pair(blocks, pair, where, held, spread):
    for b in range(blocks):
        for i in range(2):
            spread[b * TB:(b + 1) * TB, i * BLK:(i + 1) * BLK] = held[where[b, 2 * pair + i]]


def main_kernel(
    n_mp, n_dp, rows, cap, parts,
    table, where, hits, stream, enc, dec_in, enc_bias, dec_bias,
    pg_out, stream_out, gdec_out, err_out,
    lat, pg, err, dec, dec_wide, picked, picked_dec, err_wide, spread, *rest,
):
    mp = Axis("mp", n_mp)
    dp = Axis("dp", n_dp)
    per = n_mp * cap // n_dp
    part = per // parts
    blocks = n_mp * rows
    pre_bufs, dec_bufs, code_bufs, sems = rest[0:5], rest[5:10], rest[10:15], rest[15:]
    barrier = pltpu.get_barrier_semaphore()
    count = mp.greet(barrier) + dp.greet(barrier)
    empty = jnp.zeros((TB, BLK), BF16)
    lat[n_mp * cap] = empty
    pg[n_mp * cap] = empty
    pl.semaphore_wait(barrier, count)
    pending = []

    def group(i):
        return sems[4 * i:4 * i + 4]

    def home_rows(m):
        return pl.ds(m * rows, rows)

    def region(p):
        return lambda m: pl.ds(m * per + p * part, part)

    def producer(p, left, right):
        def produce(chunk, dest, place):
            def one(i, _):
                slot = chunk * per + p * part + i
                dest[place, i] = jnp.dot(
                    left[table[0, slot]], right[table[1, slot]], preferred_element_type=F32
                ).astype(dest.dtype)
                return 0

            lax.fori_loop(0, part, one, 0, unroll=True)

        return produce

    def reduce_and_gather(left, right, bufs, first, held, finish, aside, work):
        sums = [
            scatter_sum(
                dp,
                producer(p, left, right),
                [b.at[p] for b in bufs],
                group(first + p),
                pending,
            )
            for p in range(parts)
        ]
        for _ in range(dp.fars):
            next(sums[0])
        for p in range(parts):
            for _ in range(dp.fars):
                if p + 1 < parts:
                    next(sums[p + 1])
                next(sums[p])
        aside(0)
        for p in range(parts):
            total = next(sums[p])
            for i in range(part):
                slot = dp.me * per + p * part + i
                held[slot] = finish(slot, total[i])
            gather_start(dp, held, region(p), group(first + parts + p), pending)
            if p + 1 < parts:
                aside(p + 1)
        for p in range(parts):
            gather_forward(
                dp, held, region(p), group(first + parts + p), pending, functools.partial(work, p)
            )
        for p in range(parts):
            gather_finish(dp, held, region(p), group(first + parts + p))

    def activate(slot, pre_sum):
        shifted = pre_sum + enc_bias[table[1, slot]]
        live = jnp.sum(hits[slot], axis=0, keepdims=True)
        return (jnp.maximum(shifted, 0.0) * live).astype(BF16)

    def turn_dec(p):
        for k in range(p * LBLK_DEV // parts, (p + 1) * LBLK_DEV // parts):
            dec[k] = dec_in[:, k * BLK:(k + 1) * BLK].T

    def split_dec(p, step):
        calls = parts * dp.fars
        at = p * dp.fars + step
        for k in range(at * LBLK_DEV // calls, (at + 1) * LBLK_DEV // calls):
            dec_wide[k] = dec_in[:, k * BLK:(k + 1) * BLK]

    reduce_and_gather(stream, enc, pre_bufs, 0, lat, activate, turn_dec, split_dec)

    def produce_dec(home, dest, place):
        for c in range(cap):
            slot = home * cap + c
            picked_dec[c * BLK:(c + 1) * BLK, :] = dec[table[1, slot]]
            block = lat[slot]
            for j in range(rows):
                hit = jnp.broadcast_to(hits[slot, j:j + 1], (TB, BLK)).astype(BF16)
                picked[j * TB:(j + 1) * TB, c * BLK:(c + 1) * BLK] = block * hit
        out = jnp.dot(picked[...], picked_dec[...], preferred_element_type=F32)
        dest[place] = out.reshape(dest.shape[1:]).astype(dest.dtype)

    sums = scatter_sum(mp, produce_dec, dec_bufs, group(4 * parts), pending)
    for _ in range(2 * mp.fars):
        next(sums)
    recon = next(sums) + dec_bias[...][None]
    mine = (recon - stream[home_rows(mp.me)].astype(F32)).astype(BF16)
    err[home_rows(mp.me)] = mine
    gather_start(mp, err, home_rows, group(4 * parts + 1), pending)
    for j in range(rows):
        err_out[:, j * TB:(j + 1) * TB] = mine[j].T
    for b in range(blocks):
        stream_out[:, b * TB:(b + 1) * TB] = stream[b].T
    gather_forward(mp, err, home_rows, group(4 * parts + 1), pending)
    gather_finish(mp, err, home_rows, group(4 * parts + 1))

    def to_pre_grad(slot, code):
        on = lat[slot].astype(F32) > 0
        return jnp.where(on, code * (1.0 / TB), 0.0).astype(BF16)

    def turn_err(p):
        for b in range(p * blocks // parts, (p + 1) * blocks // parts):
            err_wide[:, b * TB:(b + 1) * TB] = err[b].T

    def grad_dec(p, step):
        calls = parts * dp.fars
        at = p * dp.fars + step
        pairs = LBLK_DEV // 2

        def one(pair, _):
            spread_pair(blocks, pair, where, lat, spread)
            total = jnp.dot(err_wide[...], spread[...], preferred_element_type=F32)
            lane = pl.multiple_of(pair * 2 * BLK, 2 * BLK)
            gdec_out[:, pl.ds(lane, 2 * BLK)] = (total * (1.0 / TB)).astype(BF16)
            return 0

        if at * pairs // calls < (at + 1) * pairs // calls:
            lax.fori_loop(at * pairs // calls, (at + 1) * pairs // calls, one, 0)

    reduce_and_gather(err, dec_wide, code_bufs, 2 * parts, pg, to_pre_grad, turn_err, grad_dec)
    pg_out[...] = pg[...]
    for copy in pending:
        copy.wait_send()


def grad_kernel(blocks, where, stream, pg, gdec_in, err_in, genc, gbias, gdec, err, spread):
    gdec[...] = gdec_in[...]

    @pl.when(pl.program_id(0) == 0)
    def _():
        err[...] = err_in[...]

    spread_pair(blocks, pl.program_id(0), where, pg, spread)
    genc[...] = jnp.dot(stream[...], spread[...], preferred_element_type=F32).astype(BF16)
    gbias[...] = jnp.sum(spread[...].astype(F32), axis=0, keepdims=True)


def local(n_mp, n_dp, stream, active_lists, enc_weight, enc_bias, dec_weight, dec_bias):
    tok_count, feat = stream.shape
    rows = tok_count // TB
    cap = max(2, 16 * rows // n_mp)
    slots = n_mp * cap
    per = slots // n_dp
    parts = 2 if per % 2 == 0 else 1
    chunk = (parts, n_dp // 2, per // parts, TB, BLK)
    blocks = n_mp * rows
    mps, dps = n_mp // 2, n_dp // 2
    vmem = pl.BlockSpec(memory_space=pltpu.VMEM)
    smem = pl.BlockSpec(memory_space=pltpu.SMEM)
    dma = pltpu.SemaphoreType.DMA
    shape = jax.ShapeDtypeStruct

    lists = jnp.full((1, 8, 128), -1, jnp.int32).at[0, :rows, :LIST].set(active_lists)
    stream_all, lists_all, enc_blocks = pl.pallas_call(
        functools.partial(gather_kernel, n_mp, rows),
        out_shape=(
            shape((blocks, TB, feat), BF16),
            shape((n_mp, 8, 128), jnp.int32),
            shape((LBLK_DEV, feat, BLK), BF16),
        ),
        in_specs=[vmem] * 3,
        out_specs=(vmem,) * 3,
        scratch_shapes=[
            pltpu.VMEM((blocks, TB, feat), BF16),
            pltpu.VMEM((n_mp, 8, 128), jnp.int32),
        ] + [dma((mps,))] * 8,
        compiler_params=pltpu.CompilerParams(
            collective_id=0, has_side_effects=True, vmem_limit_bytes=VMEM_BYTES
        ),
    )(stream.T, lists, enc_weight)

    ids = lists_all[:, :rows, :LIST].reshape(n_mp, rows * LIST)
    entry = jnp.arange(rows * LIST)
    mine = (ids >= 0) & (ids // LBLK_DEV == lax.axis_index("mp"))
    before = jnp.sum(mine[:, None, :] & (entry[None, :] < entry[:, None])[None], axis=2)
    placed = mine[:, None, :] & (before[:, None, :] == jnp.arange(cap)[None, :, None])
    home = jnp.arange(n_mp)[:, None, None] * rows
    table = jnp.stack([
        jnp.sum(jnp.where(placed, entry // LIST, 0), axis=2) + home[:, :, 0],
        jnp.sum(jnp.where(placed, (ids % LBLK_DEV)[:, None, :], 0), axis=2),
    ]).reshape(2, slots).astype(jnp.int32)
    in_row = (entry // LIST)[None, :] == jnp.arange(rows)[:, None]
    hits = jnp.sum((placed[:, :, None, :] & in_row).astype(F32), axis=3)
    hits = jnp.broadcast_to(hits.reshape(slots, rows, 1), (slots, rows, BLK))

    held = placed[:, :, None, :] & in_row
    held = held[..., None] & (ids % LBLK_DEV == jnp.arange(LBLK_DEV)[:, None, None]).transpose(1, 2, 0)[
        :, None, None
    ]
    number = jnp.arange(slots).reshape(n_mp, cap, 1, 1, 1)
    where = slots - jnp.sum(jnp.where(held, slots - number, 0), axis=(1, 3))
    where = where.reshape(blocks, LBLK_DEV).astype(jnp.int32)

    small = (TB, BLK)
    wide = (rows, TB, feat)
    pg, stream_wide, grad_dec, errors = pl.pallas_call(
        functools.partial(main_kernel, n_mp, n_dp, rows, cap, parts),
        out_shape=(
            shape((slots + 1,) + small, BF16),
            shape((feat, blocks * TB), BF16),
            shape((feat, LBLK_DEV * BLK), BF16),
            shape((feat, tok_count), BF16),
        ),
        in_specs=[smem] * 2 + [vmem] * 6,
        out_specs=(vmem,) * 4,
        scratch_shapes=[
            pltpu.VMEM((slots + 1,) + small, BF16),
            pltpu.VMEM((slots + 1,) + small, BF16),
            pltpu.VMEM((blocks, TB, feat), BF16),
            pltpu.VMEM((LBLK_DEV, BLK, feat), BF16),
            pltpu.VMEM((LBLK_DEV, feat, BLK), BF16),
            pltpu.VMEM((tok_count, cap * BLK), BF16),
            pltpu.VMEM((cap * BLK, feat), BF16),
            pltpu.VMEM((feat, blocks * TB), BF16),
            pltpu.VMEM((blocks * TB, 2 * BLK), BF16),
        ]
        + [pltpu.VMEM(chunk, F32)] * 5
        + [pltpu.VMEM((mps,) + wide, t) for t in (BF16, F32, BF16, BF16, BF16)]
        + [pltpu.VMEM(chunk, t) for t in (BF16, F32, BF16, BF16, BF16)]
        + [dma((dps,))] * (16 * parts) + [dma((mps,))] * 8,
        compiler_params=pltpu.CompilerParams(
            collective_id=1, has_side_effects=True, vmem_limit_bytes=VMEM_BYTES
        ),
    )(
        table,
        where,
        hits,
        stream_all,
        enc_blocks,
        dec_weight.T,
        enc_bias.reshape(LBLK_DEV, 1, BLK),
        dec_bias.reshape(1, feat),
    )

    pair = pl.BlockSpec((feat, 2 * BLK), lambda i: (0, i))
    whole = pl.BlockSpec((feat, tok_count), lambda i: (0, 0))
    grad_enc, grad_bias, grad_dec, errors = pl.pallas_call(
        functools.partial(grad_kernel, blocks),
        grid=(LBLK_DEV // 2,),
        out_shape=(
            shape((feat, LBLK_DEV * BLK), BF16),
            shape((1, LBLK_DEV * BLK), F32),
            shape((feat, LBLK_DEV * BLK), BF16),
            shape((feat, tok_count), BF16),
        ),
        in_specs=[smem] + [vmem] * 2 + [pair, whole],
        out_specs=(pair, pl.BlockSpec((1, 2 * BLK), lambda i: (0, i)), pair, whole),
        scratch_shapes=[pltpu.VMEM((blocks * TB, 2 * BLK), BF16)],
        compiler_params=pltpu.CompilerParams(vmem_limit_bytes=VMEM_BYTES),
    )(where, stream_wide, pg, grad_dec, errors)
    return (grad_enc, grad_bias.reshape(LBLK_DEV * BLK), grad_dec.T, errors.T)


def solution(mesh):
    return jax.shard_map(
        functools.partial(local, mesh.shape["mp"], mesh.shape["dp"]),
        mesh=mesh,
        in_specs=(
            P(("groups", "mp"), "dp"),
            P(("groups", "mp"), None),
            P("dp", "mp"),
            P("mp"),
            P("mp", "dp"),
            P("dp"),
        ),
        out_specs=(
            P(("groups", "dp"), "mp"),
            P(("groups", "mp")),
            P(("groups", "mp"), "dp"),
            P(("groups", "mp"), "dp"),
        ),
        check_vma=False,
    )
```
